32 devices in a mesh: groups: 2 (over x), queue: 8 (over z, y), heads: 2 (over core).
Axes of the slice: x: 2, y: 2, z: 4, core: 2. Of those that a mesh axis runs over, the one named last changes fastest.
Arguments:
- latents: bfloat16 [6144, 3072], P(('groups', 'queue')), parts along dimension 0, may hold values from -6 to 6
- fresh: bfloat16 [768, 3072], P('groups'), parts along dimension 0, may hold values from -6 to 6
- queries: bfloat16 [1536, 3072], P(('groups', 'queue', 'heads')), parts along dimension 0, may hold values from -80 to 80
- key_weight: bfloat16 [3072, 3072], P(None, 'heads'), may hold values from -0.109375 to 0.109375
- value_weight: bfloat16 [3072, 3072], P(None, 'heads'), may hold values from -0.109375 to 0.109375
- modulation: float32 [50, 2, 3072], replicated, may hold values from -3 to 3
- frame_level: int32 [16], P('groups'), parts along dimension 0, may hold values from 0 to 49
- slot_frame: int32 [16], P('groups'), parts along dimension 0, may hold values from 0 to 7, each once
Outputs:
- attended: bfloat16 [1536, 3072], P(('groups', 'queue', 'heads')), parts along dimension 0
The draws below stay inside these ranges and needn't reach their ends.
There are 2 independent parts, one for each index of `groups`. The reference program is written for one: setup_inputs(seed, part) draws one part's arguments, and reference() takes and returns one part's arrays. A program takes and returns all parts, laid end to end along the dimension named above; an argument that names none is the same for every part. Nothing has to cross between parts.
Inputs may be any that keep to these rules, and one draw needn't show every extreme that they name: `slot_frame`: each frame sits in exactly one slot.
All inputs are finite; a program needn't handle non-finite values.
Results may differ from the reference program's by a relative error of at most 0.0055.
The reference program's roundings to bfloat16 on the way count: a program that leaves them out, or rounds other values in their place, can miss the bound.
Values may be sent and summed in bfloat16 or wider, within the bound.
A program may use at most 192 MiB of HBM per device.

```python
import jax
import jax.numpy as jnp
from jax import lax

D = 3072
ATTN_HEADS = 48
HEAD_DIM = 64
LEVELS = 50
TOK_SLOT = 384
QROWS = 96
SLOTS = 8


def draw_queries(key, part):
    key = jax.random.fold_in(key, 7)
    first, second = jax.random.split(key)
    rows = SLOTS * QROWS
    base = jnp.clip(jax.random.normal(first, (rows, D), jnp.float32), -8.0, 8.0)
    scales = jnp.exp(jax.random.uniform(second, (rows, 1), jnp.float32, jnp.log(0.5), jnp.log(2.0)))
    return (base * scales).astype(jnp.bfloat16)


def with_ends(values, own_key, least, largest):
    place = [jax.random.randint(jax.random.fold_in(own_key, axis), (), 0, length) for axis, length in enumerate(values.shape)]
    widest = values.shape.index(max(values.shape))
    neighbour = place[:widest] + [(place[widest] + 1) % values.shape[widest]] + place[widest + 1:]
    return values.at[tuple(place)].set(least).at[tuple(neighbour)].set(largest)


def block_levels(rng, dims, cuts, low, largest):
    level, own = 1.0, jax.random.fold_in(rng, 6)
    for axis_at, blocks in cuts:
        draws = jnp.exp(jax.random.uniform(jax.random.fold_in(own, axis_at), (blocks,), jnp.float32, low / len(cuts), largest / len(cuts)))
        level = level * jnp.repeat(draws, dims[axis_at] // blocks).reshape([-1 if axis == axis_at else 1 for axis in range(len(dims))])
    return level


def centred(rng, shape, width, most, cuts=(), held_as=jnp.bfloat16):
    factor_of = block_levels(rng, shape, cuts, -0.22, 0.18) if cuts else 1.0
    drawn = jax.random.normal(rng, shape, jnp.float32) * width * factor_of
    return jnp.minimum(jnp.maximum(drawn, -most), most).astype(held_as)


def setup_inputs(seed: int = 0, part: int = 0) -> dict:
    key_list = jax.random.split(jax.random.key(seed), 9)
    part_splits = jax.random.split(jax.random.fold_in(key_list[8], part), 9)
    return {
        "latents": centred(part_splits[0], (SLOTS * TOK_SLOT, D), 1.0, 6.0, ((0, 8),)),
        "fresh": centred(part_splits[1], (TOK_SLOT, D), 1.0, 6.0),
        "queries": draw_queries(jax.random.fold_in(jax.random.fold_in(key_list[8], part), 71), part),
        "key_weight": centred(key_list[3], (D, D), D ** -0.5, 0.109375, ((1, 2),)),
        "value_weight": centred(key_list[4], (D, D), D ** -0.5, 0.109375, ((1, 2),)),
        "modulation": centred(key_list[5], (LEVELS, 2, D), 0.5, 3.0, (), jnp.float32),
        "frame_level": with_ends(jax.random.randint(part_splits[6], (SLOTS,), 0, LEVELS), jax.random.fold_in(part_splits[6], 1), 0, LEVELS - 1).astype(jnp.int32),
        "slot_frame": jax.random.permutation(part_splits[7], SLOTS).astype(jnp.int32),
    }


def reference(latents, fresh, queries, key_weight, value_weight, modulation, frame_level, slot_frame):
    moved = jnp.concatenate([fresh, latents[:(SLOTS - 1) * TOK_SLOT]], 0)
    level = frame_level[slot_frame]
    mods = modulation[level]
    field = moved.astype(jnp.float32).reshape(SLOTS, TOK_SLOT, D)
    mean = lax.optimization_barrier(jnp.mean(field, axis=2, keepdims=True))
    var = lax.optimization_barrier(jnp.mean((field - mean) ** 2, axis=2, keepdims=True))
    normed = (field - mean) * lax.rsqrt(var + 1e-06)
    mixed = normed * (1.0 + mods[:, 1][:, None, :]) + mods[:, 0][:, None, :]
    mixed = mixed.astype(jnp.bfloat16).reshape(SLOTS * TOK_SLOT, D)
    keys = jnp.dot(mixed, key_weight, preferred_element_type=jnp.float32).astype(jnp.bfloat16)
    values = jnp.dot(mixed, value_weight, preferred_element_type=jnp.float32).astype(jnp.bfloat16)
    q_heads = queries.reshape(-1, ATTN_HEADS, HEAD_DIM).transpose(1, 0, 2)
    k_heads = keys.reshape(-1, ATTN_HEADS, HEAD_DIM).transpose(1, 0, 2)
    v_heads = values.reshape(-1, ATTN_HEADS, HEAD_DIM).transpose(1, 0, 2)
    scale = 1.0 / HEAD_DIM ** 0.5

    def one_head(items):
        q_one, k_one, v_one = items
        scores = jnp.dot(q_one, k_one.T, preferred_element_type=jnp.float32) * scale
        peak = lax.optimization_barrier(jnp.max(scores, axis=1, keepdims=True))
        expo = jnp.exp(scores - peak)
        totals = lax.optimization_barrier(jnp.sum(expo, axis=1, keepdims=True))
        weighted = jnp.dot(expo.astype(jnp.bfloat16), v_one, preferred_element_type=jnp.float32)
        return weighted / totals
    outs = lax.map(one_head, (q_heads, k_heads, v_heads))
    return outs.transpose(1, 0, 2).reshape(-1, D).astype(jnp.bfloat16)
```

```python
import functools

import jax
import jax.numpy as jnp
from jax import lax
from jax.experimental import pallas as pl
from jax.experimental.pallas import tpu as pltpu
from jax.sharding import PartitionSpec as P

HEAD_DIM = 64
LANES = 128
MESH = pl.DeviceIdType.MESH


def flipped(index, mask, count):
    total, bit = 0, 1
    while bit < count:
        own = lax.rem(lax.div(index, bit), 2)
        total = total + bit * ((1 - own) if mask & bit else own)
        bit *= 2
    return total


def attend_kernel(
    ranks, q_ref, k0_ref, k1_ref, v0_ref, v1_ref, out_ref,
    part, landed, result, send_sem, recv_sem, pair_send, pair_recv,
):
    queue = lax.axis_index("queue")
    core = lax.axis_index("heads")
    rank = lax.div(queue, 2)
    side = lax.rem(queue, 2)
    rows = q_ref.shape[0] // ranks
    width = q_ref.shape[1]
    pairs = width // LANES
    half = rows // 2
    masks = [ranks - 1 - step for step in range(ranks)]
    targets = [flipped(rank, mask, ranks) for mask in masks]

    barrier = pltpu.get_barrier_semaphore()
    for target in targets[:-1]:
        pl.semaphore_signal(
            barrier, inc=1, device_id={"queue": target * 2 + side}, device_id_type=MESH
        )
    pl.semaphore_signal(barrier, inc=1, device_id={"heads": 1 - core}, device_id_type=MESH)
    pl.semaphore_wait(barrier, ranks)

    lane = lax.broadcasted_iota(jnp.int32, (rows, LANES), 1)
    low = lane < HEAD_DIM
    copies = []
    for step in range(ranks):
        base = pl.multiple_of(targets[step] * rows, 16)

        def one_pair(pair, stats, base=base, step=step):
            cols = pl.ds(pl.multiple_of(pair * LANES, LANES), LANES)
            q_two = q_ref[pl.ds(base, rows), cols].astype(jnp.float32) * (HEAD_DIM**-0.5)
            left = jnp.concatenate(
                [jnp.where(low, q_two, 0.0), jnp.where(low, 0.0, q_two)], axis=0
            ).astype(jnp.bfloat16)
            k_two = jnp.concatenate([k0_ref[:, cols], k1_ref[:, cols]], axis=0)
            v_two = jnp.concatenate([v0_ref[:, cols], v1_ref[:, cols]], axis=0)
            scores = lax.dot_general(
                left, k_two, (((1,), (1,)), ((), ())), preferred_element_type=jnp.float32
            )
            peak = jnp.max(scores, axis=1, keepdims=True)
            expo = jnp.exp(scores - peak)
            total = jnp.sum(expo, axis=1, keepdims=True)
            out = jnp.dot(expo.astype(jnp.bfloat16), v_two, preferred_element_type=jnp.float32)
            part[step, :, cols] = jnp.where(low, out[:rows], out[rows:])
            for place, column in (
                (2 * pair, peak[:rows]),
                (2 * pair + 1, peak[rows:]),
                (HEAD_DIM + 2 * pair, total[:rows]),
                (HEAD_DIM + 2 * pair + 1, total[rows:]),
            ):
                stats = jnp.where(lane == place, column, stats)
            return stats

        stats = lax.fori_loop(0, pairs, one_pair, jnp.ones((rows, LANES), jnp.float32))
        part[step, :, width:] = stats
        if step < ranks - 1:
            copy = pltpu.make_async_remote_copy(
                src_ref=part.at[step],
                dst_ref=landed.at[step],
                send_sem=send_sem.at[step],
                recv_sem=recv_sem.at[step],
                device_id={"queue": targets[step] * 2 + side},
                device_id_type=MESH,
            )
            copy.start()
            copies.append(copy)
    for copy in copies:
        copy.wait()

    pieces = [landed.at[step] for step in range(ranks - 1)] + [part.at[ranks - 1]]
    stats = [piece[:, width:] for piece in pieces]
    most = functools.reduce(jnp.maximum, stats)
    shrink = [jnp.exp(one - most) for one in stats]
    totals = functools.reduce(
        jnp.add, [s * pltpu.roll(one, HEAD_DIM, 1) for s, one in zip(shrink, stats)]
    )
    factors = [s / totals for s in shrink]
    for pair in range(pairs):
        cols = pl.ds(pair * LANES, LANES)
        terms = [
            jnp.where(low, f[:, 2 * pair : 2 * pair + 1], f[:, 2 * pair + 1 : 2 * pair + 2])
            * piece[:, cols]
            for f, piece in zip(factors, pieces)
        ]
        result[:, cols] = functools.reduce(jnp.add, terms).astype(jnp.bfloat16)

    own_cols = pl.ds(pl.multiple_of(core * width, LANES), width)
    across = pltpu.make_async_remote_copy(
        src_ref=result.at[pl.ds(pl.multiple_of((1 - core) * half, 16), half)],
        dst_ref=out_ref.at[:, own_cols],
        send_sem=pair_send,
        recv_sem=pair_recv,
        device_id={"heads": 1 - core},
        device_id_type=MESH,
    )
    across.start()
    out_ref[:, own_cols] = result[pl.ds(pl.multiple_of(core * half, 16), half), :]
    across.wait()


def attend(q, k0, k1, v0, v1, ranks):
    rows, width = q.shape[0] // ranks, q.shape[1]
    keys = k0.shape[0] * 2
    return pl.pallas_call(
        functools.partial(attend_kernel, ranks),
        out_shape=jax.ShapeDtypeStruct((rows // 2, width * 2), jnp.bfloat16),
        in_specs=[pl.BlockSpec(memory_space=pltpu.VMEM)] * 5,
        out_specs=pl.BlockSpec(memory_space=pltpu.VMEM),
        scratch_shapes=[
            pltpu.VMEM((ranks, rows, width + LANES), jnp.float32),
            pltpu.VMEM((ranks, rows, width + LANES), jnp.float32),
            pltpu.VMEM((rows, width), jnp.bfloat16),
            pltpu.SemaphoreType.DMA((ranks,)),
            pltpu.SemaphoreType.DMA((ranks,)),
            pltpu.SemaphoreType.DMA,
            pltpu.SemaphoreType.DMA,
        ],
        compiler_params=pltpu.CompilerParams(
            collective_id=0, has_side_effects=True, vmem_limit_bytes=48 * 1024 * 1024
        ),
        cost_estimate=pl.CostEstimate(
            flops=4 * q.shape[0] * keys * width,
            bytes_accessed=2 * width * (q.shape[0] + 2 * keys),
            transcendentals=q.shape[0] * keys * width // HEAD_DIM,
        ),
    )(q, k0, k1, v0, v1)


def shards(latents, fresh, queries, key_weight, value_weight, modulation, frame_level, slot_frame):
    tok = latents.shape[0]
    length = lax.axis_size("queue")
    ranks = length // 2
    place = lax.axis_index("queue")
    core = lax.axis_index("heads")
    swap_cores = [(0, 1), (1, 0)]
    swap_sides = [(i, i ^ 1) for i in range(length)]

    local_q = lax.all_to_all(queries, "heads", split_axis=1, concat_axis=0, tiled=True)
    same_side = [[2 * r + s for r in range(ranks)] for s in range(2)]
    q_all = lax.all_gather(local_q, "queue", axis=0, tiled=True, axis_index_groups=same_side)

    slot = lax.rem(place + 1, length)
    moved = jnp.where(slot == 0, fresh, latents)
    frame = lax.dynamic_index_in_dim(slot_frame, slot, 0, keepdims=False)
    level = lax.dynamic_index_in_dim(frame_level, frame, 0, keepdims=False)
    mods = lax.dynamic_index_in_dim(modulation, level, 0, keepdims=False)
    field = moved.astype(jnp.float32)
    mean = jnp.mean(field, axis=1, keepdims=True)
    var = jnp.mean((field - mean) ** 2, axis=1, keepdims=True)
    normed = (field - mean) * lax.rsqrt(var + 1e-06)
    mixed = (normed * (1.0 + mods[1][None, :]) + mods[0][None, :]).astype(jnp.bfloat16)

    own_half = lax.dynamic_slice_in_dim(mixed, core * (tok // 2), tok // 2, 0)
    other_half = lax.ppermute(own_half, "queue", swap_sides)
    sibling_half = lax.ppermute(other_half, "heads", swap_cores)
    other = jnp.concatenate([other_half, sibling_half], axis=0)

    def project(rows, weight):
        return jnp.dot(rows, weight, preferred_element_type=jnp.float32).astype(jnp.bfloat16)

    k0, v0 = project(mixed, key_weight), project(mixed, value_weight)
    k1, v1 = project(other, key_weight), project(other, value_weight)
    return attend(q_all, k0, k1, v0, v1, ranks)


def solution(mesh):
    return jax.shard_map(
        shards,
        mesh=mesh,
        in_specs=(
            P(("groups", "queue"), None),
            P("groups", None),
            P(("groups", "queue", "heads"), None),
            P(None, "heads"),
            P(None, "heads"),
            P(),
            P("groups"),
            P("groups"),
        ),
        out_specs=P(("groups", "queue", "heads"), None),
        check_vma=False,
    )
```

```python
import functools

import jax
import jax.numpy as jnp
from jax import lax
from jax.experimental import pallas as pl
from jax.experimental.pallas import tpu as pltpu
from jax.sharding import PartitionSpec as P

HEAD_DIM = 64
LANES = 128
CLUSTER = 4
MESH = pl.DeviceIdType.MESH


def flipped(index, mask, count):
    total, bit = 0, 1
    while bit < count:
        own = lax.rem(lax.div(index, bit), 2)
        total = total + bit * ((1 - own) if mask & bit else own)
        bit *= 2
    return total


def attend_kernel(ranks, kinds, *refs):
    q_ref, k_refs, v_refs = refs[0], refs[1 : 1 + kinds], refs[1 + kinds : 1 + 2 * kinds]
    (out_ref, part, part_stats, landed, landed_stats, result,
     send_sem, recv_sem, pair_send, pair_recv) = refs[1 + 2 * kinds :]
    queue = lax.axis_index("queue")
    core = lax.axis_index("heads")
    rank = lax.div(queue, CLUSTER)
    member = lax.rem(queue, CLUSTER)
    rows = q_ref.shape[0] // ranks
    width = q_ref.shape[1]
    groups, span = part.shape[1], part.shape[3]
    per_group = span // LANES
    half = rows // 2
    targets = [
        flipped(rank, ranks - 1 - step, ranks) * CLUSTER + member for step in range(ranks)
    ]

    barrier = pltpu.get_barrier_semaphore()
    for target in targets[:-1]:
        pl.semaphore_signal(barrier, inc=1, device_id={"queue": target}, device_id_type=MESH)
    pl.semaphore_signal(barrier, inc=1, device_id={"heads": 1 - core}, device_id_type=MESH)
    pl.semaphore_wait(barrier, ranks)

    lane = lax.broadcasted_iota(jnp.int32, (rows, LANES), 1)
    low = lane < HEAD_DIM
    copies = []

    def send(step, place, source, target):
        copy = pltpu.make_async_remote_copy(
            src_ref=source,
            dst_ref=target,
            send_sem=send_sem.at[step, place],
            recv_sem=recv_sem.at[step, place],
            device_id={"queue": targets[step]},
            device_id_type=MESH,
        )
        copy.start()
        copies.append(copy)

    for step in range(ranks):
        stats = jnp.ones((rows, LANES), jnp.float32)
        for group in range(groups):
            for inner in range(per_group):
                pair = group * per_group + inner
                cols = pl.ds(pair * LANES, LANES)
                q_two = q_ref[pl.ds(step * rows, rows), cols].astype(jnp.float32)
                q_two = q_two * (HEAD_DIM**-0.5)
                left = jnp.concatenate(
                    [jnp.where(low, q_two, 0.0), jnp.where(low, 0.0, q_two)], axis=0
                ).astype(jnp.bfloat16)
                k_two = jnp.concatenate([ref[:, cols] for ref in k_refs], axis=0)
                v_two = jnp.concatenate([ref[:, cols] for ref in v_refs], axis=0)
                scores = lax.dot_general(
                    left, k_two, (((1,), (1,)), ((), ())), preferred_element_type=jnp.float32
                )
                peak = jnp.max(scores, axis=1, keepdims=True)
                expo = jnp.exp(scores - peak)
                total = jnp.sum(expo, axis=1, keepdims=True)
                out = jnp.dot(
                    expo.astype(jnp.bfloat16), v_two, preferred_element_type=jnp.float32
                )
                part[step, group, :, inner * LANES : (inner + 1) * LANES] = jnp.where(
                    low, out[:rows], out[rows:]
                )
                for place, column in (
                    (2 * pair, peak[:rows]),
                    (2 * pair + 1, peak[rows:]),
                    (HEAD_DIM + 2 * pair, total[:rows]),
                    (HEAD_DIM + 2 * pair + 1, total[rows:]),
                ):
                    stats = jnp.where(lane == place, column, stats)
            if step < ranks - 1:
                send(step, group, part.at[step, group], landed.at[step, group])
        part_stats[step] = stats
        if step < ranks - 1:
            send(step, groups, part_stats.at[step], landed_stats.at[step])
    for copy in copies:
        copy.wait()

    stats = [landed_stats[step] for step in range(ranks - 1)] + [part_stats[ranks - 1]]
    pieces = [landed.at[step] for step in range(ranks - 1)] + [part.at[ranks - 1]]
    most = functools.reduce(jnp.maximum, stats)
    shrink = [jnp.exp(one - most) for one in stats]
    totals = functools.reduce(
        jnp.add, [s * pltpu.roll(one, HEAD_DIM, 1) for s, one in zip(shrink, stats)]
    )
    factors = [s / totals for s in shrink]
    for pair in range(width // LANES):
        group, inner = divmod(pair, per_group)
        terms = [
            jnp.where(low, f[:, 2 * pair : 2 * pair + 1], f[:, 2 * pair + 1 : 2 * pair + 2])
            * piece[group, :, inner * LANES : (inner + 1) * LANES]
            for f, piece in zip(factors, pieces)
        ]
        result[:, pair * LANES : (pair + 1) * LANES] = functools.reduce(jnp.add, terms).astype(
            jnp.bfloat16
        )

    own_cols = pl.ds(pl.multiple_of(core * width, LANES), width)
    across = pltpu.make_async_remote_copy(
        src_ref=result.at[pl.ds(pl.multiple_of((1 - core) * half, 16), half)],
        dst_ref=out_ref.at[:, own_cols],
        send_sem=pair_send,
        recv_sem=pair_recv,
        device_id={"heads": 1 - core},
        device_id_type=MESH,
    )
    across.start()
    out_ref[:, own_cols] = result[pl.ds(pl.multiple_of(core * half, 16), half), :]
    across.wait()


def attend(q, k_list, v_list, ranks):
    rows, width = q.shape[0] // ranks, q.shape[1]
    keys = sum(k.shape[0] for k in k_list)
    groups = 4
    blocks = pltpu.VMEM((ranks, groups, rows, width // groups), jnp.float32)
    notes = pltpu.VMEM((ranks, rows, LANES), jnp.float32)
    return pl.pallas_call(
        functools.partial(attend_kernel, ranks, len(k_list)),
        out_shape=jax.ShapeDtypeStruct((rows // 2, width * 2), jnp.bfloat16),
        in_specs=[pl.BlockSpec(memory_space=pltpu.VMEM)] * (1 + 2 * len(k_list)),
        out_specs=pl.BlockSpec(memory_space=pltpu.VMEM),
        scratch_shapes=[
            blocks, notes, blocks, notes,
            pltpu.VMEM((rows, width), jnp.bfloat16),
            pltpu.SemaphoreType.DMA((ranks, groups + 1)),
            pltpu.SemaphoreType.DMA((ranks, groups + 1)),
            pltpu.SemaphoreType.DMA,
            pltpu.SemaphoreType.DMA,
        ],
        compiler_params=pltpu.CompilerParams(
            collective_id=0, has_side_effects=True, vmem_limit_bytes=48 * 1024 * 1024
        ),
        cost_estimate=pl.CostEstimate(
            flops=4 * q.shape[0] * keys * width,
            bytes_accessed=2 * width * (q.shape[0] + 2 * keys),
            transcendentals=q.shape[0] * keys * width // HEAD_DIM,
        ),
    )(q, *k_list, *v_list)


def shards(latents, fresh, queries, key_weight, value_weight, modulation, frame_level, slot_frame):
    tok = latents.shape[0]
    length = lax.axis_size("queue")
    ranks = length // CLUSTER
    place = lax.axis_index("queue")
    core = lax.axis_index("heads")

    def to_queue(rows, mask):
        return lax.ppermute(rows, "queue", [(i, i ^ mask) for i in range(length)])

    def to_sibling(rows):
        return lax.ppermute(rows, "heads", [(0, 1), (1, 0)])

    slot = lax.rem(place + 1, length)
    moved = jnp.where(slot == 0, fresh, latents)
    frame = lax.dynamic_index_in_dim(slot_frame, slot, 0, keepdims=False)
    level = lax.dynamic_index_in_dim(frame_level, frame, 0, keepdims=False)
    mods = lax.dynamic_index_in_dim(modulation, level, 0, keepdims=False)
    field = moved.astype(jnp.float32)
    mean = jnp.mean(field, axis=1, keepdims=True)
    var = jnp.mean((field - mean) ** 2, axis=1, keepdims=True)
    normed = (field - mean) * lax.rsqrt(var + 1e-06)
    mixed = (normed * (1.0 + mods[1][None, :]) + mods[0][None, :]).astype(jnp.bfloat16)

    own_half = lax.dynamic_slice_in_dim(mixed, core * (tok // 2), tok // 2, 0)
    from_one = to_queue(own_half, 1)
    from_two = to_queue(own_half, 2)
    near = jnp.concatenate([from_one, from_two], axis=0)
    diagonal = jnp.concatenate(
        [to_queue(from_one[: tok // 4], 2), to_queue(from_two[tok // 4 :], 1)], axis=0
    )
    near = jnp.concatenate([near, to_sibling(near)], axis=0)
    diagonal = jnp.concatenate([diagonal, to_sibling(diagonal)], axis=0)

    width = queries.shape[1] // 2
    kept = lax.dynamic_slice_in_dim(queries, core * width, width, 1)
    given = to_sibling(lax.dynamic_slice_in_dim(queries, (1 - core) * width, width, 1))
    local_q = jnp.where(
        core == 0,
        jnp.concatenate([kept, given], axis=0),
        jnp.concatenate([given, kept], axis=0),
    )
    q_steps = [to_queue(local_q, CLUSTER * mask) for mask in range(ranks - 1, 0, -1)]
    q_all = jnp.concatenate(q_steps + [local_q], axis=0)

    def project(rows, weight):
        return jnp.dot(rows, weight, preferred_element_type=jnp.float32).astype(jnp.bfloat16)

    sources = (mixed, near, diagonal)
    k_list = [project(rows, key_weight) for rows in sources]
    v_list = [project(rows, value_weight) for rows in sources]
    return attend(q_all, k_list, v_list, ranks)


def solution(mesh):
    return jax.shard_map(
        shards,
        mesh=mesh,
        in_specs=(
            P(("groups", "queue"), None),
            P("groups", None),
            P(("groups", "queue", "heads"), None),
            P(None, "heads"),
            P(None, "heads"),
            P(),
            P("groups"),
            P("groups"),
        ),
        out_specs=P(("groups", "queue", "heads"), None),
        check_vma=False,
    )
```

```python
import functools

import jax
import jax.numpy as jnp
from jax import lax
from jax.experimental import pallas as pl
from jax.experimental.pallas import tpu as pltpu
from jax.sharding import PartitionSpec as P

HEAD_DIM = 64
LANES = 128
CLUSTER = 4
MESH = pl.DeviceIdType.MESH


def flipped(index, mask, count):
    total, bit = 0, 1
    while bit < count:
        own = lax.rem(lax.div(index, bit), 2)
        total = total + bit * ((1 - own) if mask & bit else own)
        bit *= 2
    return total


def attend_kernel(ranks, kinds, *refs):
    q_ref, k_refs, v_refs = refs[0], refs[1 : 1 + kinds], refs[1 + kinds : 1 + 2 * kinds]
    (out_ref, part, part_stats, landed, landed_stats, result,
     send_sem, recv_sem, pair_send, pair_recv) = refs[1 + 2 * kinds :]
    queue = lax.axis_index("queue")
    core = lax.axis_index("heads")
    rank = lax.div(queue, CLUSTER)
    member = lax.rem(queue, CLUSTER)
    rows = q_ref.shape[0] // ranks
    width = q_ref.shape[1]
    groups, span = part.shape[1], part.shape[3]
    per_group = span // LANES
    half = rows // 2
    targets = [
        flipped(rank, ranks - 1 - step, ranks) * CLUSTER + member for step in range(ranks)
    ]

    barrier = pltpu.get_barrier_semaphore()
    for target in targets[:-1]:
        pl.semaphore_signal(barrier, inc=1, device_id={"queue": target}, device_id_type=MESH)
    pl.semaphore_signal(barrier, inc=1, device_id={"heads": 1 - core}, device_id_type=MESH)
    pl.semaphore_wait(barrier, ranks)

    lane = lax.broadcasted_iota(jnp.int32, (rows, LANES), 1)
    low = lane < HEAD_DIM
    copies = []

    def send(step, place, source, target):
        copy = pltpu.make_async_remote_copy(
            src_ref=source,
            dst_ref=target,
            send_sem=send_sem.at[step, place],
            recv_sem=recv_sem.at[step, place],
            device_id={"queue": targets[step]},
            device_id_type=MESH,
        )
        copy.start()
        copies.append(copy)

    for step in range(ranks):
        stats = jnp.ones((rows, LANES), jnp.float32)
        for group in range(groups):
            for inner in range(per_group):
                pair = group * per_group + inner
                cols = pl.ds(pair * LANES, LANES)
                q_two = q_ref[pl.ds(step * rows, rows), cols].astype(jnp.float32)
                q_two = q_two * (HEAD_DIM**-0.5)
                left = jnp.concatenate(
                    [jnp.where(low, q_two, 0.0), jnp.where(low, 0.0, q_two)], axis=0
                ).astype(jnp.bfloat16)
                k_two = jnp.concatenate([ref[:, cols] for ref in k_refs], axis=0)
                v_two = jnp.concatenate([ref[:, cols] for ref in v_refs], axis=0)
                scores = lax.dot_general(
                    left, k_two, (((1,), (1,)), ((), ())), preferred_element_type=jnp.float32
                )
                peak = jnp.max(scores, axis=1, keepdims=True)
                expo = jnp.exp(scores - peak)
                total = jnp.sum(expo, axis=1, keepdims=True)
                out = jnp.dot(
                    expo.astype(jnp.bfloat16), v_two, preferred_element_type=jnp.float32
                )
                part[step, group, :, inner * LANES : (inner + 1) * LANES] = jnp.where(
                    low, out[:rows], out[rows:]
                )
                for place, column in (
                    (2 * pair, peak[:rows]),
                    (2 * pair + 1, peak[rows:]),
                    (HEAD_DIM + 2 * pair, total[:rows]),
                    (HEAD_DIM + 2 * pair + 1, total[rows:]),
                ):
                    stats = jnp.where(lane == place, column, stats)
            if step < ranks - 1:
                send(step, group, part.at[step, group], landed.at[step, group])
        part_stats[step] = stats
        if step < ranks - 1:
            send(step, groups, part_stats.at[step], landed_stats.at[step])
    for copy in copies:
        copy.wait()

    stats = [landed_stats[step] for step in range(ranks - 1)] + [part_stats[ranks - 1]]
    pieces = [landed.at[step] for step in range(ranks - 1)] + [part.at[ranks - 1]]
    most = functools.reduce(jnp.maximum, stats)
    shrink = [jnp.exp(one - most) for one in stats]
    totals = functools.reduce(
        jnp.add, [s * pltpu.roll(one, HEAD_DIM, 1) for s, one in zip(shrink, stats)]
    )
    factors = [s / totals for s in shrink]
    for pair in range(width // LANES):
        group, inner = divmod(pair, per_group)
        terms = [
            jnp.where(low, f[:, 2 * pair : 2 * pair + 1], f[:, 2 * pair + 1 : 2 * pair + 2])
            * piece[group, :, inner * LANES : (inner + 1) * LANES]
            for f, piece in zip(factors, pieces)
        ]
        result[:, pair * LANES : (pair + 1) * LANES] = functools.reduce(jnp.add, terms).astype(
            jnp.bfloat16
        )

    own_cols = pl.ds(pl.multiple_of(core * width, LANES), width)
    across = pltpu.make_async_remote_copy(
        src_ref=result.at[pl.ds(pl.multiple_of((1 - core) * half, 16), half)],
        dst_ref=out_ref.at[:, own_cols],
        send_sem=pair_send,
        recv_sem=pair_recv,
        device_id={"heads": 1 - core},
        device_id_type=MESH,
    )
    across.start()
    out_ref[:, own_cols] = result[pl.ds(pl.multiple_of(core * half, 16), half), :]
    across.wait()


def attend(q, k_list, v_list, ranks):
    rows, width = q.shape[0] // ranks, q.shape[1]
    keys = sum(k.shape[0] for k in k_list)
    groups = 4
    blocks = pltpu.VMEM((ranks, groups, rows, width // groups), jnp.float32)
    notes = pltpu.VMEM((ranks, rows, LANES), jnp.float32)
    return pl.pallas_call(
        functools.partial(attend_kernel, ranks, len(k_list)),
        out_shape=jax.ShapeDtypeStruct((rows // 2, width * 2), jnp.bfloat16),
        in_specs=[pl.BlockSpec(memory_space=pltpu.VMEM)] * (1 + 2 * len(k_list)),
        out_specs=pl.BlockSpec(memory_space=pltpu.VMEM),
        scratch_shapes=[
            blocks, notes, blocks, notes,
            pltpu.VMEM((rows, width), jnp.bfloat16),
            pltpu.SemaphoreType.DMA((ranks, groups + 1)),
            pltpu.SemaphoreType.DMA((ranks, groups + 1)),
            pltpu.SemaphoreType.DMA,
            pltpu.SemaphoreType.DMA,
        ],
        compiler_params=pltpu.CompilerParams(
            collective_id=0, has_side_effects=True, vmem_limit_bytes=48 * 1024 * 1024
        ),
        cost_estimate=pl.CostEstimate(
            flops=4 * q.shape[0] * keys * width,
            bytes_accessed=2 * width * (q.shape[0] + 2 * keys),
            transcendentals=q.shape[0] * keys * width // HEAD_DIM,
        ),
    )(q, *k_list, *v_list)


def norm_kernel(slot_ref, frame_ref, level_ref, latents_ref, fresh_ref, mods_ref, out_ref):
    field = jnp.where(slot_ref[0] == 0, fresh_ref[...], latents_ref[...]).astype(jnp.float32)
    mean = jnp.mean(field, axis=1, keepdims=True)
    centred = field - mean
    var = jnp.mean(centred * centred, axis=1, keepdims=True)
    normed = centred * lax.rsqrt(var + 1e-06)
    out_ref[...] = (normed * (1.0 + mods_ref[0, 1:2, :]) + mods_ref[0, 0:1, :]).astype(jnp.bfloat16)


def normed_rows(latents, fresh, modulation, slot_frame, frame_level, slot):
    rows, width = latents.shape
    block = rows // 4

    def from_latents(i, slot, frame, level):
        return jnp.where(slot[0] == 0, 0, i), 0

    def from_fresh(i, slot, frame, level):
        return jnp.where(slot[0] == 0, i, 0), 0

    return pl.pallas_call(
        norm_kernel,
        out_shape=jax.ShapeDtypeStruct((rows, width), jnp.bfloat16),
        grid_spec=pltpu.PrefetchScalarGridSpec(
            num_scalar_prefetch=3,
            grid=(4,),
            in_specs=[
                pl.BlockSpec((block, width), from_latents),
                pl.BlockSpec((block, width), from_fresh),
                pl.BlockSpec(
                    (1, 2, width), lambda i, slot, frame, level: (level[frame[slot[0]]], 0, 0)
                ),
            ],
            out_specs=pl.BlockSpec((block, width), lambda i, slot, frame, level: (i, 0)),
        ),
        compiler_params=pltpu.CompilerParams(vmem_limit_bytes=32 * 1024 * 1024),
        cost_estimate=pl.CostEstimate(
            flops=8 * rows * width, bytes_accessed=6 * rows * width, transcendentals=rows
        ),
    )(slot.reshape(1).astype(jnp.int32), slot_frame, frame_level, latents, fresh, modulation)


def shards(latents, fresh, queries, key_weight, value_weight, modulation, frame_level, slot_frame):
    tok = latents.shape[0]
    length = lax.axis_size("queue")
    ranks = length // CLUSTER
    place = lax.axis_index("queue")
    core = lax.axis_index("heads")

    def to_queue(rows, mask):
        return lax.ppermute(rows, "queue", [(i, i ^ mask) for i in range(length)])

    def to_sibling(rows):
        return lax.ppermute(rows, "heads", [(0, 1), (1, 0)])

    slot = lax.rem(place + 1, length)
    mixed = normed_rows(latents, fresh, modulation, slot_frame, frame_level, slot)

    own_half = lax.dynamic_slice_in_dim(mixed, core * (tok // 2), tok // 2, 0)
    from_one = to_queue(own_half, 1)
    from_two = to_queue(own_half, 2)
    near = jnp.concatenate([from_one, from_two], axis=0)
    near_too = to_sibling(near)
    diagonal = jnp.concatenate(
        [to_queue(from_one[: tok // 4], 2), to_queue(from_two[tok // 4 :], 1)], axis=0
    )

    width = queries.shape[1] // 2
    kept = lax.dynamic_slice_in_dim(queries, core * width, width, 1)
    given = to_sibling(lax.dynamic_slice_in_dim(queries, (1 - core) * width, width, 1))
    local_q = jnp.where(
        core == 0,
        jnp.concatenate([kept, given], axis=0),
        jnp.concatenate([given, kept], axis=0),
    )
    q_steps = [to_queue(local_q, CLUSTER * mask) for mask in range(ranks - 1, 0, -1)]
    q_all = jnp.concatenate(q_steps + [local_q], axis=0)

    def project(rows, weight):
        return jnp.dot(rows, weight, preferred_element_type=jnp.float32).astype(jnp.bfloat16)

    def both(rows):
        return project(rows, key_weight), project(rows, value_weight)

    pairs = [both(mixed), both(near)]
    diagonal, pairs[1] = lax.optimization_barrier((diagonal, pairs[1]))
    diagonal = jnp.concatenate([diagonal, to_sibling(diagonal)], axis=0)
    pairs.append(both(near_too))
    diagonal, pairs[2] = lax.optimization_barrier((diagonal, pairs[2]))
    pairs.append(both(diagonal))
    k_list, v_list = zip(*pairs)
    return attend(q_all, k_list, v_list, ranks)


def solution(mesh):
    return jax.shard_map(
        shards,
        mesh=mesh,
        in_specs=(
            P(("groups", "queue"), None),
            P("groups", None),
            P(("groups", "queue", "heads"), None),
            P(None, "heads"),
            P(None, "heads"),
            P(),
            P("groups"),
            P("groups"),
        ),
        out_specs=P(("groups", "queue", "heads"), None),
        check_vma=False,
    )
```

```python
import functools

import jax
import jax.numpy as jnp
from jax import lax
from jax.experimental import pallas as pl
from jax.experimental.pallas import tpu as pltpu
from jax.sharding import PartitionSpec as P

HEAD_DIM = 64
LANES = 128
CLUSTER = 4
MESH = pl.DeviceIdType.MESH


def flipped(index, mask, count):
    total, bit = 0, 1
    while bit < count:
        own = lax.rem(lax.div(index, bit), 2)
        total = total + bit * ((1 - own) if mask & bit else own)
        bit *= 2
    return total


def attend_kernel(ranks, kinds, *refs):
    q_ref, k_refs, v_refs = refs[0], refs[1 : 1 + kinds], refs[1 + kinds : 1 + 2 * kinds]
    (out_ref, part, part_stats, landed, landed_stats, result,
     send_sem, recv_sem, pair_send, pair_recv) = refs[1 + 2 * kinds :]
    queue = lax.axis_index("queue")
    core = lax.axis_index("heads")
    rank = lax.div(queue, CLUSTER)
    member = lax.rem(queue, CLUSTER)
    rows = q_ref.shape[0] // ranks
    width = q_ref.shape[1]
    groups, span = part.shape[1], part.shape[3]
    per_group = span // LANES
    half = rows // 2
    targets = [
        flipped(rank, ranks - 1 - step, ranks) * CLUSTER + member for step in range(ranks)
    ]

    barrier = pltpu.get_barrier_semaphore()
    for target in targets[:-1]:
        pl.semaphore_signal(barrier, inc=1, device_id={"queue": target}, device_id_type=MESH)
    pl.semaphore_signal(barrier, inc=1, device_id={"heads": 1 - core}, device_id_type=MESH)
    pl.semaphore_wait(barrier, ranks)

    lane = lax.broadcasted_iota(jnp.int32, (rows, LANES), 1)
    low = lane < HEAD_DIM
    copies = []

    def send(step, place, source, target):
        copy = pltpu.make_async_remote_copy(
            src_ref=source,
            dst_ref=target,
            send_sem=send_sem.at[step, place],
            recv_sem=recv_sem.at[step, place],
            device_id={"queue": targets[step]},
            device_id_type=MESH,
        )
        copy.start()
        copies.append(copy)

    for step in range(ranks):
        stats = jnp.ones((rows, LANES), jnp.float32)
        for group in range(groups):
            for inner in range(per_group):
                pair = group * per_group + inner
                cols = pl.ds(pair * LANES, LANES)
                q_two = q_ref[pl.ds(step * rows, rows), cols].astype(jnp.float32)
                q_two = q_two * (HEAD_DIM**-0.5)
                left = jnp.concatenate(
                    [jnp.where(low, q_two, 0.0), jnp.where(low, 0.0, q_two)], axis=0
                ).astype(jnp.bfloat16)
                k_two = jnp.concatenate([ref[:, cols] for ref in k_refs], axis=0)
                v_two = jnp.concatenate([ref[:, cols] for ref in v_refs], axis=0)
                scores = lax.dot_general(
                    left, k_two, (((1,), (1,)), ((), ())), preferred_element_type=jnp.float32
                )
                peak = jnp.max(scores, axis=1, keepdims=True)
                expo = jnp.exp(scores - peak)
                total = jnp.sum(expo, axis=1, keepdims=True)
                out = jnp.dot(
                    expo.astype(jnp.bfloat16), v_two, preferred_element_type=jnp.float32
                )
                part[step, group, :, inner * LANES : (inner + 1) * LANES] = jnp.where(
                    low, out[:rows], out[rows:]
                )
                for place, column in (
                    (2 * pair, peak[:rows]),
                    (2 * pair + 1, peak[rows:]),
                    (HEAD_DIM + 2 * pair, total[:rows]),
                    (HEAD_DIM + 2 * pair + 1, total[rows:]),
                ):
                    stats = jnp.where(lane == place, column, stats)
            if step < ranks - 1:
                send(step, group, part.at[step, group], landed.at[step, group])
        part_stats[step] = stats
        if step < ranks - 1:
            send(step, groups, part_stats.at[step], landed_stats.at[step])
    for copy in copies:
        copy.wait()

    stats = [landed_stats[step] for step in range(ranks - 1)] + [part_stats[ranks - 1]]
    pieces = [landed.at[step] for step in range(ranks - 1)] + [part.at[ranks - 1]]
    most = functools.reduce(jnp.maximum, stats)
    shrink = [jnp.exp(one - most) for one in stats]
    totals = functools.reduce(
        jnp.add, [s * pltpu.roll(one, HEAD_DIM, 1) for s, one in zip(shrink, stats)]
    )
    factors = [s / totals for s in shrink]
    for pair in range(width // LANES):
        group, inner = divmod(pair, per_group)
        terms = [
            jnp.where(low, f[:, 2 * pair : 2 * pair + 1], f[:, 2 * pair + 1 : 2 * pair + 2])
            * piece[group, :, inner * LANES : (inner + 1) * LANES]
            for f, piece in zip(factors, pieces)
        ]
        result[:, pair * LANES : (pair + 1) * LANES] = functools.reduce(jnp.add, terms).astype(
            jnp.bfloat16
        )

    own_cols = pl.ds(pl.multiple_of(core * width, LANES), width)
    across = pltpu.make_async_remote_copy(
        src_ref=result.at[pl.ds(pl.multiple_of((1 - core) * half, 16), half)],
        dst_ref=out_ref.at[:, own_cols],
        send_sem=pair_send,
        recv_sem=pair_recv,
        device_id={"heads": 1 - core},
        device_id_type=MESH,
    )
    across.start()
    out_ref[:, own_cols] = result[pl.ds(pl.multiple_of(core * half, 16), half), :]
    across.wait()


def attend(q, k_list, v_list, ranks):
    rows, width = q.shape[0] // ranks, q.shape[1]
    keys = sum(k.shape[0] for k in k_list)
    groups = 4
    blocks = pltpu.VMEM((ranks, groups, rows, width // groups), jnp.float32)
    notes = pltpu.VMEM((ranks, rows, LANES), jnp.float32)
    return pl.pallas_call(
        functools.partial(attend_kernel, ranks, len(k_list)),
        out_shape=jax.ShapeDtypeStruct((rows // 2, width * 2), jnp.bfloat16),
        in_specs=[pl.BlockSpec(memory_space=pltpu.VMEM)] * (1 + 2 * len(k_list)),
        out_specs=pl.BlockSpec(memory_space=pltpu.VMEM),
        scratch_shapes=[
            blocks, notes, blocks, notes,
            pltpu.VMEM((rows, width), jnp.bfloat16),
            pltpu.SemaphoreType.DMA((ranks, groups + 1)),
            pltpu.SemaphoreType.DMA((ranks, groups + 1)),
            pltpu.SemaphoreType.DMA,
            pltpu.SemaphoreType.DMA,
        ],
        compiler_params=pltpu.CompilerParams(
            collective_id=0, has_side_effects=True, vmem_limit_bytes=48 * 1024 * 1024
        ),
        cost_estimate=pl.CostEstimate(
            flops=4 * q.shape[0] * keys * width,
            bytes_accessed=2 * width * (q.shape[0] + 2 * keys),
            transcendentals=q.shape[0] * keys * width // HEAD_DIM,
        ),
    )(q, *k_list, *v_list)


def norm_kernel(slot_ref, frame_ref, level_ref, latents_ref, fresh_ref, mods_ref, out_ref):
    field = jnp.where(slot_ref[0] == 0, fresh_ref[...], latents_ref[...]).astype(jnp.float32)
    mean = jnp.mean(field, axis=1, keepdims=True)
    centred = field - mean
    var = jnp.mean(centred * centred, axis=1, keepdims=True)
    normed = centred * lax.rsqrt(var + 1e-06)
    out_ref[...] = (normed * (1.0 + mods_ref[0, 1:2, :]) + mods_ref[0, 0:1, :]).astype(jnp.bfloat16)


def normed_rows(latents, fresh, modulation, slot_frame, frame_level, slot):
    rows, width = latents.shape
    block = rows // 4

    def from_latents(i, slot, frame, level):
        return jnp.where(slot[0] == 0, 0, i), 0

    def from_fresh(i, slot, frame, level):
        return jnp.where(slot[0] == 0, i, 0), 0

    return pl.pallas_call(
        norm_kernel,
        out_shape=jax.ShapeDtypeStruct((rows, width), jnp.bfloat16),
        grid_spec=pltpu.PrefetchScalarGridSpec(
            num_scalar_prefetch=3,
            grid=(4,),
            in_specs=[
                pl.BlockSpec((block, width), from_latents),
                pl.BlockSpec((block, width), from_fresh),
                pl.BlockSpec(
                    (1, 2, width), lambda i, slot, frame, level: (level[frame[slot[0]]], 0, 0)
                ),
            ],
            out_specs=pl.BlockSpec((block, width), lambda i, slot, frame, level: (i, 0)),
        ),
        compiler_params=pltpu.CompilerParams(vmem_limit_bytes=32 * 1024 * 1024),
        cost_estimate=pl.CostEstimate(
            flops=8 * rows * width, bytes_accessed=6 * rows * width, transcendentals=rows
        ),
    )(slot.reshape(1).astype(jnp.int32), slot_frame, frame_level, latents, fresh, modulation)


def shards(latents, fresh, queries, key_weight, value_weight, modulation, frame_level, slot_frame):
    tok = latents.shape[0]
    length = lax.axis_size("queue")
    ranks = length // CLUSTER
    place = lax.axis_index("queue")
    core = lax.axis_index("heads")

    def to_queue(rows, mask):
        return lax.ppermute(rows, "queue", [(i, i ^ mask) for i in range(length)])

    def to_sibling(rows):
        return lax.ppermute(rows, "heads", [(0, 1), (1, 0)])

    slot = lax.rem(place + 1, length)
    mixed = normed_rows(latents, fresh, modulation, slot_frame, frame_level, slot)

    own_half = lax.dynamic_slice_in_dim(mixed, core * (tok // 2), tok // 2, 0)
    from_one = to_queue(own_half, 1)
    from_two = to_queue(own_half, 2)
    def project(rows, weight):
        return jnp.dot(rows, weight, preferred_element_type=jnp.float32).astype(jnp.bfloat16)

    def both(rows):
        return project(rows, key_weight), project(rows, value_weight)

    own = both(mixed)
    from_one, from_two, own = lax.optimization_barrier((from_one, from_two, own))
    near = jnp.concatenate([from_one, from_two], axis=0)
    near_too = to_sibling(near)
    diagonal = jnp.concatenate(
        [to_queue(from_one[: tok // 4], 2), to_queue(from_two[tok // 4 :], 1)], axis=0
    )

    width = queries.shape[1] // 2
    kept = lax.dynamic_slice_in_dim(queries, core * width, width, 1)
    given = to_sibling(lax.dynamic_slice_in_dim(queries, (1 - core) * width, width, 1))
    local_q = jnp.where(
        core == 0,
        jnp.concatenate([kept, given], axis=0),
        jnp.concatenate([given, kept], axis=0),
    )
    q_steps = [to_queue(local_q, CLUSTER * mask) for mask in range(ranks - 1, 0, -1)]
    q_all = jnp.concatenate(q_steps + [local_q], axis=0)

    pairs = [own, both(near)]
    diagonal, pairs[1] = lax.optimization_barrier((diagonal, pairs[1]))
    diagonal = jnp.concatenate([diagonal, to_sibling(diagonal)], axis=0)
    pairs.append(both(near_too))
    diagonal, pairs[2] = lax.optimization_barrier((diagonal, pairs[2]))
    pairs.append(both(diagonal))
    k_list, v_list = zip(*pairs)
    return attend(q_all, k_list, v_list, ranks)


def solution(mesh):
    return jax.shard_map(
        shards,
        mesh=mesh,
        in_specs=(
            P(("groups", "queue"), None),
            P("groups", None),
            P(("groups", "queue", "heads"), None),
            P(None, "heads"),
            P(None, "heads"),
            P(),
            P("groups"),
            P("groups"),
        ),
        out_specs=P(("groups", "queue", "heads"), None),
        check_vma=False,
    )
```
